32 devices in a mesh: req: 4 (over y, core), voc: 8 (over z, x).
Axes of the slice: x: 2, y: 2, z: 4, core: 2. Of those that a mesh axis runs over, the one named last changes fastest.
Arguments:
- hidden: bfloat16 [4096, 1536], P(('req', 'voc')), may hold values from -64 to 64
- norm_gain: float32 [1536], replicated, may hold values from 0.1 to 1.9
- head: bfloat16 [1536, 49152], P(None, 'voc'), may hold values from -8 to 8
- targets: int32 [4096], P(('req', 'voc')), may hold values from 0 to 49151
- bounds: int32 [32, 2], P(('req', 'voc')), may hold values from 0 to 128, as said below
Outputs:
- logprob: float32 [4096], P(('req', 'voc'))
- entropy: float32 [4096], P(('req', 'voc'))
- target_logit: float32 [4096], P(('req', 'voc'))
- mean_entropy: float32 [1], replicated
The draws below stay inside these ranges and needn't reach their ends.
Inputs may be any that keep to these rules, and one draw needn't show every extreme that they name: bounds[d] = (lo, hi): slots lo to hi - 1 of device d hold live response rows; 1 <= hi - lo <= 96, lo <= 32; some device has hi - lo = 96 and hi = 128, some has lo = 0.
All inputs are finite; a program needn't handle non-finite values.
Results may differ from the reference program's by a relative error of at most 0.00075.
The reference program's roundings to bfloat16 on the way (of `normed`) count: a program that leaves them out, or rounds other values in their place, can miss the bound.
Values may be sent and summed in bfloat16 or wider, within the bound.
A program may use at most 64 MiB of HBM per device.

```python
import math
import jax
import jax.numpy as jnp
import numpy as np
from jax import lax

D = 1536
VOCAB = 49152
ROW_DEV = 128
LIVE = 96
ROWS = 4096


def live_bounds(key):
    inner = jax.random.fold_in(key, 5)
    first_key, second_key = jax.random.split(inner)
    ndev = ROWS // ROW_DEV
    start = jax.random.randint(first_key, (ndev,), 0, ROW_DEV - LIVE + 1)
    counts = jax.random.randint(second_key, (ndev,), max(1, LIVE // 3), LIVE + 1)
    start = start.at[0].set(ROW_DEV - LIVE).at[1].set(0)
    counts = counts.at[0].set(LIVE)
    return jnp.stack([start, start + counts], axis=1).astype(jnp.int32)


def aligned_base(key):
    signs = jnp.where(jax.random.bernoulli(jax.random.fold_in(key, 77), 0.5, (8, D)), 1.0, -1.0)
    sizes = jax.random.uniform(jax.random.fold_in(key, 78), (8, D), jnp.float32, 0.8, 1.2)
    return signs * sizes * D ** (-0.5)


def row_plan(key):
    direction = jnp.clip(jax.random.normal(jax.random.fold_in(key, 11), (ROWS, D), jnp.float32), -4.0, 4.0)
    owned = jax.random.permutation(jax.random.fold_in(key, 12), VOCAB)[:ROWS].astype(jnp.int32)
    strength = 0.8 * jnp.exp(jax.random.uniform(jax.random.fold_in(key, 13), (ROWS,), jnp.float32) * math.log(10.0))
    return (direction, owned, strength)


def draw_bounds(key, part):
    return live_bounds(key)


def draw_head(key, part):
    weights = jax.random.normal(jax.random.fold_in(key, 1), (D, VOCAB), jnp.float32) * D ** (-0.5)
    weights = jnp.clip(weights, -6.0 * D ** (-0.5), 6.0 * D ** (-0.5))
    direction, owned, strength = row_plan(key)
    weights = weights.at[:, owned].set((direction * (strength[:, None] * D ** (-0.5))).T)
    base = aligned_base(key)
    level = 110.0 + jnp.arange(8, dtype=jnp.float32) * 30.0
    first = jnp.arange(8, dtype=jnp.int32) * (VOCAB // 8) + 5
    second = first + VOCAB // 16
    weights = weights.at[:, first].set((base * (level[:, None] / math.sqrt(D))).T)
    weights = weights.at[:, second].set((base * ((level[:, None] - 2.0) / math.sqrt(D))).T)
    return weights.astype(jnp.bfloat16)


def draw_hidden(key, part):
    noise = jnp.clip(jax.random.normal(jax.random.fold_in(key, 2), (ROWS, D), jnp.float32), -4.0, 4.0)
    direction, owned, strength = row_plan(key)
    values = (noise + 1.5 * direction) / 1.8
    ndev = ROWS // ROW_DEV
    bounds = live_bounds(key)
    owners = jnp.arange(8, dtype=jnp.int32) * ndev // 8
    chosen = owners * ROW_DEV + bounds[owners, 0]
    values = values.at[chosen].set(aligned_base(key) * 3.0)
    return values.astype(jnp.bfloat16)


def touch_ends(entries, key, low, top_value):
    place = [jax.random.randint(jax.random.fold_in(key, axis), (), 0, length) for axis, length in enumerate(entries.shape)]
    widest = entries.shape.index(max(entries.shape))
    neighbour = place[:widest] + [(place[widest] + 1) % entries.shape[widest]] + place[widest + 1:]
    return entries.at[tuple(place)].set(low).at[tuple(neighbour)].set(top_value)


def rank_table(number_of, skew):
    portions = [(1 << 20) // math.isqrt(grade ** skew) + 1 for grade in range(1, number_of + 1)]
    scale = 1 + sum(portions) // (1 << 30)
    return np.cumsum(np.array([max(1, weight // scale) for weight in portions]))


def ranked(own_key, extent, amount, slope):
    grid = rank_table(amount, slope)
    ticket = jax.random.randint(jax.random.fold_in(own_key, 1), extent, 0, int(grid[amount - 1]))
    rank = jnp.searchsorted(jnp.asarray(grid, jnp.int32), ticket, side="right")
    return jax.random.permutation(jax.random.fold_in(own_key, 2), amount)[rank].astype(jnp.int32)


def setup_inputs(seed: int = 0) -> dict:
    seeds = jax.random.split(jax.random.key(seed), 6)
    return {
        "hidden": draw_hidden(jax.random.fold_in(seeds[5], 71), 0),
        "norm_gain": jnp.clip(1.0 + 0.18 * jax.random.normal(seeds[1], (D,), jnp.float32), 0.1, 1.9),
        "head": draw_head(jax.random.fold_in(seeds[5], 71), 0),
        "targets": touch_ends(ranked(seeds[3], (ROWS,), VOCAB, 2), jax.random.fold_in(seeds[3], 3), 0, VOCAB - 1).astype(jnp.int32),
        "bounds": draw_bounds(jax.random.fold_in(seeds[5], 71), 0),
    }


def pick_block(count):
    size = min(count, 512)
    while count % size:
        size -= 1
    return size

def reference(hidden, norm_gain, head, targets, bounds):
    values = hidden.astype(jnp.float32)
    meansq = lax.optimization_barrier(jnp.mean(values * values, axis=-1, keepdims=True))
    normed = (values * lax.rsqrt(meansq + 1e-05) * norm_gain).astype(jnp.bfloat16)
    block = pick_block(ROWS)
    columns = jnp.arange(VOCAB, dtype=jnp.int32)

    def one_block(pair):
        rows_in, ids = pair
        logits = jnp.dot(rows_in, head, preferred_element_type=jnp.float32)
        top = lax.optimization_barrier(jnp.max(logits, axis=-1))
        expo = jnp.exp(logits - top[:, None])
        total = lax.optimization_barrier(jnp.sum(expo, axis=-1))
        weighted = lax.optimization_barrier(jnp.sum(expo * logits, axis=-1))
        picked = lax.optimization_barrier(jnp.sum(jnp.where(columns[None, :] == ids[:, None], logits, 0.0), axis=-1))
        return (top, total, weighted, picked)
    top, total, weighted, picked = lax.map(one_block, (normed.reshape(ROWS // block, block, D), targets.reshape(ROWS // block, block)))
    top, total, weighted, picked = [a.reshape(ROWS) for a in (top, total, weighted, picked)]
    lse = top + jnp.log(total)
    index = jnp.arange(ROWS, dtype=jnp.int32)
    owner = index // ROW_DEV
    slot = index % ROW_DEV
    live = (slot >= bounds[owner, 0]) & (slot < bounds[owner, 1])
    zero = jnp.zeros((ROWS,), jnp.float32)
    entropy = jnp.where(live, lse - weighted / total, zero)
    logprob = jnp.where(live, picked - lse, zero)
    target_logit = jnp.where(live, picked, zero)
    mean_entropy = (jnp.sum(entropy) / jnp.sum(live.astype(jnp.float32))).reshape(1)
    return (logprob, entropy, target_logit, mean_entropy)
```

```python
import functools

import jax
import jax.numpy as jnp
from jax import lax
from jax.experimental import pallas as pl
from jax.experimental.pallas import tpu as pltpu
from jax.sharding import PartitionSpec as P

LIVE = 96
SIDE = 2
LANES = 128
CHUNK = 768
LOW = -1e30


def kernel(
    nreq, nvoc, bounds, hidden, gain, targets, head, logprob, entropy, picked_out, mean,
    rows, weights, first, second, top, total, weighted, picked, group,
    meta, stats, stats_out, ent, ent_sum,
    head_sem, rows_rx, down_tx, up_tx, side_tx, meta_rx, meta_tx, stats_rx, stats_tx,
    ent_rx, ent_tx, sum_rx, sum_tx,
):
    nz = nvoc // SIDE
    req = lax.axis_index("req")
    me = lax.axis_index("voc")
    x = lax.rem(me, SIDE)
    z = me // SIDE
    partner = z * SIDE + (SIDE - 1 - x)
    slots = hidden.shape[0]
    width = head.shape[1]
    chunks = width // CHUNK
    cells = CHUNK // LANES

    def at(place, side):
        return place * SIDE + side

    def load_head(c):
        return pltpu.make_async_copy(
            head.at[:, pl.ds(pl.multiple_of(c * CHUNK, CHUNK), CHUNK)], weights.at[c], head_sem.at[c]
        )

    barrier = pltpu.get_barrier_semaphore()
    for i in range(1, nvoc):
        pl.semaphore_signal(barrier, inc=1, device_id={"voc": lax.rem(me + i, nvoc)})
    for i in range(1, nreq):
        pl.semaphore_signal(barrier, inc=1, device_id={"req": lax.rem(req + i, nreq)})

    for c in range(chunks):
        load_head(c).start()

    lo = bounds[0, 0]
    hi = bounds[0, 1]
    values = hidden[...].astype(jnp.float32)
    meansq = jnp.mean(values * values, axis=-1, keepdims=True)
    normed = (values * lax.rsqrt(meansq + 1e-05) * gain[...]).astype(jnp.bfloat16)
    slot = lax.broadcasted_iota(jnp.int32, (LIVE, slots), 1)
    order = lax.broadcasted_iota(jnp.int32, (LIVE, slots), 0)
    window = jnp.where(slot == order + lo, 1.0, 0.0).astype(jnp.bfloat16)
    rows[me] = jnp.dot(window, normed, preferred_element_type=jnp.float32).astype(jnp.bfloat16)
    tile_row = lax.broadcasted_iota(jnp.int32, (8, slots), 0)
    meta[me] = jnp.where(tile_row == 0, jnp.broadcast_to(targets[...], (8, slots)), lo)

    pl.semaphore_wait(barrier, nvoc - 1 + nreq - 1)

    def send_rows(source, target, sem):
        return pltpu.make_async_remote_copy(
            src_ref=rows.at[source], dst_ref=rows.at[source], send_sem=sem,
            recv_sem=rows_rx.at[source], device_id={"voc": target},
        )

    def send_down(place):
        return send_rows(at(place, x), at(z - 1, x), down_tx.at[place])

    def send_up(place):
        return send_rows(at(place, x), at(z + 1, x), up_tx.at[place])

    def send_side(place):
        return send_rows(at(place, x), partner, side_tx.at[place])

    def send_meta(i):
        return pltpu.make_async_remote_copy(
            src_ref=meta.at[me], dst_ref=meta.at[me], send_sem=meta_tx.at[i],
            recv_sem=meta_rx.at[me], device_id={"voc": lax.rem(me + i, nvoc)},
        )

    @pl.when(z > 0)
    def _():
        send_down(z).start()

    @pl.when(z < nz - 1)
    def _():
        send_up(z).start()

    send_side(z).start()
    for i in range(1, nvoc):
        send_meta(i).start()

    def local_ids(block):
        ids = jnp.broadcast_to(meta[block, 0:1, :], (LIVE, slots))
        start = jnp.broadcast_to(meta[block, 1:2, :], (LIVE, slots))
        hit = slot == order + start
        id_column = jnp.sum(jnp.where(hit, ids, 0).astype(jnp.float32), axis=-1, keepdims=True)
        return id_column.astype(jnp.int32) - me * width, hit

    def prepare(blocks):
        for n, block in enumerate(blocks):
            ids, _ = local_ids(block)
            group[pl.ds(n * LIVE, LIVE), :] = jnp.broadcast_to(ids >> 7, (LIVE, LANES))
        size = len(blocks) * LIVE
        top[pl.ds(0, size), :] = jnp.full((size, LANES), LOW, jnp.float32)
        for state in (total, weighted, picked):
            state[pl.ds(0, size), :] = jnp.zeros((size, LANES), jnp.float32)

    def multiply(blocks, c, out):
        left = [rows[block] for block in blocks]
        left = left[0] if len(left) == 1 else jnp.concatenate(left, axis=0)
        out[pl.ds(0, len(blocks) * LIVE), :] = jnp.dot(
            left, weights[c], preferred_element_type=jnp.float32
        )

    def absorb(count, c, logits):
        for r in range(0, count * LIVE, 8):
            here = pl.ds(r, 8)
            part = [logits[here, pl.ds(j * LANES, LANES)] for j in range(cells)]
            old = top[here, :]
            new = functools.reduce(jnp.maximum, part, old)
            scale = jnp.exp(old - new)
            expo = [jnp.exp(v - new) for v in part]
            top[here, :] = new
            total[here, :] = total[here, :] * scale + functools.reduce(jnp.add, expo)
            weighted[here, :] = weighted[here, :] * scale + functools.reduce(
                jnp.add, [e * v for e, v in zip(expo, part)]
            )
            wanted = group[here, :]
            found = picked[here, :]
            for j, v in enumerate(part):
                found = jnp.where(wanted == c * cells + j, v, found)
            picked[here, :] = found

    def block_stats(n, block):
        here = pl.ds(n * LIVE, LIVE)
        ids, hit = local_ids(block)
        best = jnp.max(top[here, :], axis=-1, keepdims=True)
        scale = jnp.exp(top[here, :] - best)
        lane = lax.broadcasted_iota(jnp.int32, (LIVE, LANES), 1)
        columns = (
            best,
            jnp.sum(total[here, :] * scale, axis=-1, keepdims=True),
            jnp.sum(weighted[here, :] * scale, axis=-1, keepdims=True),
            jnp.sum(jnp.where(lane == (ids & 127), picked[here, :], 0.0), axis=-1, keepdims=True),
        )
        lines = [jnp.sum(jnp.where(hit, col, 0.0), axis=0, keepdims=True) for col in columns]
        return jnp.concatenate(lines + [jnp.zeros((4, slots), jnp.float32)], axis=0)

    def work(blocks, fresh):
        def ready(c):
            if fresh:
                load_head(c).wait()

        prepare(blocks)
        ready(0)
        multiply(blocks, 0, first)

        def body(i, carry):
            c = i * 2
            ready(c + 1)
            multiply(blocks, c + 1, second)
            absorb(len(blocks), c, first)
            ready(c + 2)
            multiply(blocks, c + 2, first)
            absorb(len(blocks), c + 1, second)
            return carry

        lax.fori_loop(0, chunks // 2 - 1, body, 0)
        ready(chunks - 1)
        multiply(blocks, chunks - 1, second)
        absorb(len(blocks), chunks - 2, first)
        absorb(len(blocks), chunks - 1, second)

    def send_stats(block):
        return pltpu.make_async_remote_copy(
            src_ref=stats_out.at[block], dst_ref=stats.at[me], send_sem=stats_tx.at[block],
            recv_sem=stats_rx.at[me], device_id={"voc": block},
        )

    def give(n, block):
        stats_out[block] = block_stats(n, block)
        send_stats(block).start()

    def wait_meta(block):
        pltpu.make_async_remote_copy(
            src_ref=meta.at[block], dst_ref=meta.at[block], send_sem=meta_tx.at[0],
            recv_sem=meta_rx.at[block], device_id={"voc": partner},
        ).wait_recv()

    def wait_rows(block):
        send_rows(block, partner, side_tx.at[0]).wait_recv()

    near = jnp.minimum(z, nz - 1 - z)
    far_side = jnp.where(z > nz - 1 - z, -1, 1)

    def line(i):
        close = i < 2 * near
        step = jnp.where(close, i // 2 + 1, i - near + 1)
        side = jnp.where(close, 2 * lax.rem(i, 2) - 1, far_side)
        return z + side * step

    work([me], True)
    stats[me] = block_stats(0, me)

    def tick(t, carry):
        @pl.when(z - t >= 0)
        def _():
            wait_rows(at(z - t, x))

            @pl.when(z < nz - 1)
            def _():
                send_up(z - t).start()

            send_side(z - t).start()

        @pl.when(z + t < nz)
        def _():
            wait_rows(at(z + t, x))

            @pl.when(z > 0)
            def _():
                send_down(z + t).start()

            send_side(z + t).start()

        across = at(jnp.where(t == 1, z, line(jnp.maximum(t - 2, 0))), SIDE - 1 - x)
        along = at(line(t - 1), x)
        wait_rows(across)
        wait_meta(across)
        wait_meta(along)
        work([across, along], False)
        give(0, across)
        give(1, along)
        return carry

    lax.fori_loop(1, nz, tick, 0)
    last = at(line(nz - 2), SIDE - 1 - x)
    wait_rows(last)
    wait_meta(last)
    work([last], False)
    give(0, last)

    for i in range(1, nvoc):
        source = lax.rem(me + i, nvoc)
        pltpu.make_async_remote_copy(
            src_ref=stats_out.at[source], dst_ref=stats.at[source], send_sem=stats_tx.at[source],
            recv_sem=stats_rx.at[source], device_id={"voc": source},
        ).wait_recv()
    tiles = [stats[i] for i in range(nvoc)]
    best = functools.reduce(jnp.maximum, [tile[0:1] for tile in tiles])
    scales = [jnp.exp(tile[0:1] - best) for tile in tiles]
    all_total = functools.reduce(jnp.add, [tile[1:2] * s for tile, s in zip(tiles, scales)])
    all_weighted = functools.reduce(jnp.add, [tile[2:3] * s for tile, s in zip(tiles, scales)])
    chosen = functools.reduce(jnp.add, [tile[3:4] for tile in tiles])
    place = lax.broadcasted_iota(jnp.int32, (1, slots), 1)
    live = (place >= lo) & (place < hi)
    lse = best + jnp.log(all_total)
    row_entropy = jnp.where(live, lse - all_weighted / all_total, 0.0)
    logprob[...] = jnp.where(live, chosen - lse, 0.0)
    entropy[...] = row_entropy
    picked_out[...] = jnp.where(live, chosen, 0.0)

    ent[me] = jnp.concatenate(
        [row_entropy, jnp.where(live, 1.0, 0.0), jnp.zeros((6, slots), jnp.float32)], axis=0
    )

    def send_ent(i):
        return pltpu.make_async_remote_copy(
            src_ref=ent.at[me], dst_ref=ent.at[me], send_sem=ent_tx.at[i],
            recv_sem=ent_rx.at[me], device_id={"voc": lax.rem(me + i, nvoc)},
        )

    def send_sum(i):
        return pltpu.make_async_remote_copy(
            src_ref=ent_sum.at[req], dst_ref=ent_sum.at[req], send_sem=sum_tx.at[i],
            recv_sem=sum_rx.at[req], device_id={"req": lax.rem(req + i, nreq)},
        )

    for i in range(1, nvoc):
        send_ent(i).start()
    for i in range(1, nvoc):
        source = lax.rem(me + i, nvoc)
        pltpu.make_async_remote_copy(
            src_ref=ent.at[source], dst_ref=ent.at[source], send_sem=ent_tx.at[i],
            recv_sem=ent_rx.at[source], device_id={"voc": source},
        ).wait_recv()
    ent_sum[req] = functools.reduce(jnp.add, [ent[i] for i in range(nvoc)])
    for i in range(1, nreq):
        send_sum(i).start()
    for i in range(1, nreq):
        source = lax.rem(req + i, nreq)
        pltpu.make_async_remote_copy(
            src_ref=ent_sum.at[source], dst_ref=ent_sum.at[source], send_sem=sum_tx.at[i],
            recv_sem=sum_rx.at[source], device_id={"req": source},
        ).wait_recv()
    summed = jnp.sum(functools.reduce(jnp.add, [ent_sum[i] for i in range(nreq)]), axis=-1, keepdims=True)
    mean[...] = summed[0:1] / summed[1:2]

    for place in range(nz):
        send_side(place).wait_send()

        @pl.when((z > 0) & (z <= place))
        def _():
            send_down(place).wait_send()

        @pl.when((z < nz - 1) & (z >= place))
        def _():
            send_up(place).wait_send()

    for i in range(1, nvoc):
        send_meta(i).wait_send()
        send_stats(lax.rem(me + i, nvoc)).wait_send()
        send_ent(i).wait_send()
    for i in range(1, nreq):
        send_sum(i).wait_send()


def shards(nreq, nvoc, hidden, norm_gain, head, targets, bounds):
    slots, depth = hidden.shape
    width = head.shape[1]
    nz = nvoc // SIDE
    chunks = width // CHUNK
    pair = 2 * LIVE
    vmem = pl.BlockSpec(memory_space=pltpu.VMEM)
    line = jax.ShapeDtypeStruct((1, slots), jnp.float32)
    dma = pltpu.SemaphoreType.DMA
    outs = pl.pallas_call(
        functools.partial(kernel, nreq, nvoc),
        out_shape=(line, line, line, jax.ShapeDtypeStruct((1, 1), jnp.float32)),
        in_specs=[
            pl.BlockSpec(memory_space=pltpu.SMEM), vmem, vmem, vmem, pl.BlockSpec(memory_space=pl.ANY),
        ],
        out_specs=(vmem, vmem, vmem, vmem),
        scratch_shapes=[
            pltpu.VMEM((nvoc, LIVE, depth), jnp.bfloat16),
            pltpu.VMEM((chunks, depth, CHUNK), jnp.bfloat16),
            pltpu.VMEM((pair, CHUNK), jnp.float32),
            pltpu.VMEM((pair, CHUNK), jnp.float32),
            pltpu.VMEM((pair, LANES), jnp.float32),
            pltpu.VMEM((pair, LANES), jnp.float32),
            pltpu.VMEM((pair, LANES), jnp.float32),
            pltpu.VMEM((pair, LANES), jnp.float32),
            pltpu.VMEM((pair, LANES), jnp.int32),
            pltpu.VMEM((nvoc, 8, slots), jnp.int32),
            pltpu.VMEM((nvoc, 8, slots), jnp.float32),
            pltpu.VMEM((nvoc, 8, slots), jnp.float32),
            pltpu.VMEM((nvoc, 8, slots), jnp.float32),
            pltpu.VMEM((nreq, 8, slots), jnp.float32),
            dma((chunks,)),
            dma((nvoc,)),
            dma((nz,)),
            dma((nz,)),
            dma((nz,)),
            dma((nvoc,)),
            dma((nvoc,)),
            dma((nvoc,)),
            dma((nvoc,)),
            dma((nvoc,)),
            dma((nvoc,)),
            dma((nreq,)),
            dma((nreq,)),
        ],
        compiler_params=pltpu.CompilerParams(
            collective_id=0, has_side_effects=True, vmem_limit_bytes=48 * 1024 * 1024
        ),
        cost_estimate=pl.CostEstimate(
            flops=2 * nvoc * LIVE * depth * width,
            bytes_accessed=2 * depth * width,
            transcendentals=nvoc * LIVE * width,
        ),
    )(bounds, hidden, norm_gain.reshape(1, depth), targets.reshape(1, slots), head)
    return tuple(a.reshape(-1) for a in outs)


def solution(mesh):
    placed = (
        P(("req", "voc"), None),
        P(),
        P(None, "voc"),
        P(("req", "voc")),
        P(("req", "voc"), None),
    )
    return jax.shard_map(
        functools.partial(shards, mesh.shape["req"], mesh.shape["voc"]),
        mesh=mesh,
        in_specs=placed,
        out_specs=(P(("req", "voc")), P(("req", "voc")), P(("req", "voc")), P()),
        check_vma=False,
    )
```

```python
import functools

import jax
import jax.numpy as jnp
from jax import lax
from jax.experimental import pallas as pl
from jax.experimental.pallas import tpu as pltpu
from jax.sharding import PartitionSpec as P

LIVE = 96
HALF = LIVE // 2
SIDE = 2
LANES = 128
CHUNK = 768
LOW = -1e30


def kernel(
    nreq, nvoc, hidden_in, gain_in, targets_in, bounds_in, head, out,
    hidden, gain, targets, bounds, rows, weights, first, second, top, total, weighted, picked, group,
    meta, stats, stats_out, ent, ent_sum,
    in_sem, head_sem, rows_rx, down_tx, up_tx, side_tx, extra_tx, meta_rx, meta_tx, stats_rx, stats_tx,
    ent_rx, ent_tx, sum_rx, sum_tx,
):
    nz = nvoc // SIDE
    req = lax.axis_index("req")
    me = lax.axis_index("voc")
    x = lax.rem(me, SIDE)
    z = me // SIDE
    partner = z * SIDE + (SIDE - 1 - x)
    slots = hidden.shape[0]
    width = head.shape[1]
    chunks = width // CHUNK
    cells = CHUNK // LANES

    def at(place, side):
        return place * SIDE + side

    def load_head(c):
        return pltpu.make_async_copy(
            head.at[:, pl.ds(pl.multiple_of(c * CHUNK, CHUNK), CHUNK)], weights.at[c], head_sem.at[c]
        )

    loads = [
        pltpu.make_async_copy(source, target, in_sem.at[n])
        for n, (source, target) in enumerate(
            ((hidden_in, hidden), (gain_in, gain), (targets_in, targets), (bounds_in, bounds))
        )
    ]
    for load in loads:
        load.start()
    barrier = pltpu.get_barrier_semaphore()
    for i in range(1, nvoc):
        pl.semaphore_signal(barrier, inc=1, device_id={"voc": lax.rem(me + i, nvoc)})
    for i in range(1, nreq):
        pl.semaphore_signal(barrier, inc=1, device_id={"req": lax.rem(req + i, nreq)})

    for c in range(chunks):
        load_head(c).start()

    for load in loads:
        load.wait()
    lo = bounds[0:1, 0:1]
    hi = bounds[0:1, 1:2]
    values = hidden[...].astype(jnp.float32)
    meansq = jnp.mean(values * values, axis=-1, keepdims=True)
    values = values * lax.rsqrt(meansq + 1e-05)
    normed = jnp.concatenate(
        [values[:, j * LANES : (j + 1) * LANES] * gain[j : j + 1, :] for j in range(gain.shape[0])],
        axis=1,
    ).astype(jnp.bfloat16)
    slot = lax.broadcasted_iota(jnp.int32, (LIVE, slots), 1)
    order = lax.broadcasted_iota(jnp.int32, (LIVE, slots), 0)
    window = jnp.where(slot == order + lo, 1.0, 0.0).astype(jnp.bfloat16)
    rows[me] = jnp.dot(window, normed, preferred_element_type=jnp.float32).astype(jnp.bfloat16)
    tile_row = lax.broadcasted_iota(jnp.int32, (8, slots), 0)
    meta[me] = jnp.where(tile_row == 0, jnp.broadcast_to(targets[...], (8, slots)), jnp.broadcast_to(lo, (8, slots)))

    pl.semaphore_wait(barrier, nvoc - 1 + nreq - 1)

    def send_rows(block, half, target, sem):
        piece = rows.at[block, pl.ds(half * HALF, HALF)]
        return pltpu.make_async_remote_copy(
            src_ref=piece, dst_ref=piece, send_sem=sem,
            recv_sem=rows_rx.at[block, half], device_id={"voc": target},
        )

    def send_down(place, half):
        return send_rows(at(place, x), half, at(z - 1, x), down_tx.at[place, half])

    def send_up(place, half):
        return send_rows(at(place, x), half, at(z + 1, x), up_tx.at[place, half])

    def send_side(place, half):
        return send_rows(at(place, x), half, partner, side_tx.at[place, half])

    def extra_up():
        return send_rows(at(0, SIDE - 1 - x), 1, at(z + 1, x), extra_tx.at[0])

    def extra_down():
        return send_rows(at(nz - 1, SIDE - 1 - x), 1, at(z - 1, x), extra_tx.at[1])

    def wait_rows(block, half):
        send_rows(block, half, partner, side_tx.at[0, 0]).wait_recv()

    def send_meta(i):
        return pltpu.make_async_remote_copy(
            src_ref=meta.at[me], dst_ref=meta.at[me], send_sem=meta_tx.at[i],
            recv_sem=meta_rx.at[me], device_id={"voc": lax.rem(me + i, nvoc)},
        )

    for half in range(2):
        @pl.when(z > 0)
        def _():
            send_down(z, half).start()

        @pl.when(z < nz - 1)
        def _():
            send_up(z, half).start()

        send_side(z, half).start()
    for i in range(1, nvoc):
        send_meta(i).start()

    def local_ids(block):
        ids = jnp.broadcast_to(meta[block, 0:1, :], (LIVE, slots))
        start = jnp.broadcast_to(meta[block, 1:2, :], (LIVE, slots))
        hit = slot == order + start
        id_column = jnp.sum(jnp.where(hit, ids, 0).astype(jnp.float32), axis=-1, keepdims=True)
        return id_column.astype(jnp.int32) - me * width, hit

    def prepare(blocks):
        for n, block in enumerate(blocks):
            ids, _ = local_ids(block)
            group[pl.ds(n * LIVE, LIVE), :] = jnp.broadcast_to(ids >> 7, (LIVE, LANES))
        size = len(blocks) * LIVE
        top[pl.ds(0, size), :] = jnp.full((size, LANES), LOW, jnp.float32)
        for state in (total, weighted, picked):
            state[pl.ds(0, size), :] = jnp.zeros((size, LANES), jnp.float32)

    def multiply(blocks, c, out):
        left = [rows[block] for block in blocks]
        left = left[0] if len(left) == 1 else jnp.concatenate(left, axis=0)
        out[pl.ds(0, len(blocks) * LIVE), :] = jnp.dot(
            left, weights[c], preferred_element_type=jnp.float32
        )

    def absorb(count, c, logits):
        for r in range(0, count * LIVE, 8):
            here = pl.ds(r, 8)
            part = [logits[here, pl.ds(j * LANES, LANES)] for j in range(cells)]
            old = top[here, :]
            new = functools.reduce(jnp.maximum, part, old)
            scale = jnp.exp(old - new)
            expo = [jnp.exp(v - new) for v in part]
            top[here, :] = new
            total[here, :] = total[here, :] * scale + functools.reduce(jnp.add, expo)
            weighted[here, :] = weighted[here, :] * scale + functools.reduce(
                jnp.add, [e * v for e, v in zip(expo, part)]
            )
            wanted = group[here, :]
            found = picked[here, :]
            for j, v in enumerate(part):
                found = jnp.where(wanted == c * cells + j, v, found)
            picked[here, :] = found

    def block_stats(n, block):
        here = pl.ds(n * LIVE, LIVE)
        ids, hit = local_ids(block)
        best = jnp.max(top[here, :], axis=-1, keepdims=True)
        scale = jnp.exp(top[here, :] - best)
        lane = lax.broadcasted_iota(jnp.int32, (LIVE, LANES), 1)
        columns = (
            best,
            jnp.sum(total[here, :] * scale, axis=-1, keepdims=True),
            jnp.sum(weighted[here, :] * scale, axis=-1, keepdims=True),
            jnp.sum(jnp.where(lane == (ids & 127), picked[here, :], 0.0), axis=-1, keepdims=True),
        )
        lines = [jnp.sum(jnp.where(hit, col, 0.0), axis=0, keepdims=True) for col in columns]
        return jnp.concatenate(lines + [jnp.zeros((4, slots), jnp.float32)], axis=0)

    def forward(t, half):
        @pl.when(z - t >= 0)
        def _():
            wait_rows(at(z - t, x), half)

            @pl.when(z < nz - 1)
            def _():
                send_up(z - t, half).start()

            @pl.when((half == 0) | (z - t > 0))
            def _():
                send_side(z - t, half).start()

        @pl.when(z + t < nz)
        def _():
            wait_rows(at(z + t, x), half)

            @pl.when(z > 0)
            def _():
                send_down(z + t, half).start()

            @pl.when((half == 0) | (z + t < nz - 1))
            def _():
                send_side(z + t, half).start()

        gap = t - 1
        due = (t == 1) if half == 1 else (t > 1)

        @pl.when(due & (z == gap))
        def _():
            wait_rows(at(0, SIDE - 1 - x), 1)
            extra_up().start()

        @pl.when(due & (nz - 1 - z == gap))
        def _():
            wait_rows(at(nz - 1, SIDE - 1 - x), 1)
            extra_down().start()

    def wait_across(place):
        block = at(place, SIDE - 1 - x)
        wait_rows(block, 0)
        inner = (place > 0) & (place < nz - 1)
        opposite = (place - z == nz - 1) | (z - place == nz - 1)

        @pl.when(inner | opposite)
        def _():
            wait_rows(block, 1)

    def work(blocks, fresh, middle=None):
        steps = chunks // 2 - 1

        def ready(c):
            if fresh:
                load_head(c).wait()

        prepare(blocks)
        ready(0)
        multiply(blocks, 0, first)

        def body(i, carry):
            if middle is not None:
                pl.when(i == min(2, steps - 1))(middle)
            c = i * 2
            ready(c + 1)
            multiply(blocks, c + 1, second)
            absorb(len(blocks), c, first)
            ready(c + 2)
            multiply(blocks, c + 2, first)
            absorb(len(blocks), c + 1, second)
            return carry

        lax.fori_loop(0, steps, body, 0)
        ready(chunks - 1)
        multiply(blocks, chunks - 1, second)
        absorb(len(blocks), chunks - 2, first)
        absorb(len(blocks), chunks - 1, second)

    def send_stats(block):
        return pltpu.make_async_remote_copy(
            src_ref=stats_out.at[block], dst_ref=stats.at[me], send_sem=stats_tx.at[block],
            recv_sem=stats_rx.at[me], device_id={"voc": block},
        )

    def give(n, block):
        stats_out[block] = block_stats(n, block)
        send_stats(block).start()

    def wait_meta(block):
        pltpu.make_async_remote_copy(
            src_ref=meta.at[block], dst_ref=meta.at[block], send_sem=meta_tx.at[0],
            recv_sem=meta_rx.at[block], device_id={"voc": partner},
        ).wait_recv()

    near = jnp.minimum(z, nz - 1 - z)
    far_side = jnp.where(z > nz - 1 - z, -1, 1)

    def line(i):
        close = i < 2 * near
        step = jnp.where(close, i // 2 + 1, i - near + 1)
        side = jnp.where(close, 2 * lax.rem(i, 2) - 1, far_side)
        return z + side * step

    work([me], True, lambda: forward(1, 0))
    stats[me] = block_stats(0, me)
    forward(1, 1)

    def tick(t, carry):
        place = jnp.where(t == 1, z, line(jnp.maximum(t - 2, 0)))
        across = at(place, SIDE - 1 - x)
        along = at(line(t - 1), x)
        wait_across(place)
        wait_meta(across)
        wait_meta(along)

        def middle():
            @pl.when(t + 1 < nz)
            def _():
                forward(t + 1, 0)

        work([across, along], False, middle)

        @pl.when(t + 1 < nz)
        def _():
            forward(t + 1, 1)

        give(0, across)
        give(1, along)
        return carry

    lax.fori_loop(1, nz, tick, 0)
    last = at(line(nz - 2), SIDE - 1 - x)
    wait_across(line(nz - 2))
    wait_meta(last)
    work([last], False)
    give(0, last)

    for i in range(1, nvoc):
        source = lax.rem(me + i, nvoc)
        pltpu.make_async_remote_copy(
            src_ref=stats_out.at[source], dst_ref=stats.at[source], send_sem=stats_tx.at[source],
            recv_sem=stats_rx.at[source], device_id={"voc": source},
        ).wait_recv()
    tiles = [stats[i] for i in range(nvoc)]
    best = functools.reduce(jnp.maximum, [tile[0:1] for tile in tiles])
    scales = [jnp.exp(tile[0:1] - best) for tile in tiles]
    all_total = functools.reduce(jnp.add, [tile[1:2] * s for tile, s in zip(tiles, scales)])
    all_weighted = functools.reduce(jnp.add, [tile[2:3] * s for tile, s in zip(tiles, scales)])
    chosen = functools.reduce(jnp.add, [tile[3:4] for tile in tiles])
    place = lax.broadcasted_iota(jnp.int32, (1, slots), 1)
    live = (place >= lo) & (place < hi)
    lse = best + jnp.log(all_total)
    row_entropy = jnp.where(live, lse - all_weighted / all_total, 0.0)
    row_logprob = jnp.where(live, chosen - lse, 0.0)
    row_picked = jnp.where(live, chosen, 0.0)

    ent[me] = jnp.concatenate(
        [row_entropy, jnp.where(live, 1.0, 0.0), jnp.zeros((6, slots), jnp.float32)], axis=0
    )

    def send_ent(i):
        return pltpu.make_async_remote_copy(
            src_ref=ent.at[me], dst_ref=ent.at[me], send_sem=ent_tx.at[i],
            recv_sem=ent_rx.at[me], device_id={"voc": lax.rem(me + i, nvoc)},
        )

    def send_sum(i):
        return pltpu.make_async_remote_copy(
            src_ref=ent_sum.at[req], dst_ref=ent_sum.at[req], send_sem=sum_tx.at[i],
            recv_sem=sum_rx.at[req], device_id={"req": lax.rem(req + i, nreq)},
        )

    for i in range(1, nvoc):
        send_ent(i).start()
    for i in range(1, nvoc):
        source = lax.rem(me + i, nvoc)
        pltpu.make_async_remote_copy(
            src_ref=ent.at[source], dst_ref=ent.at[source], send_sem=ent_tx.at[i],
            recv_sem=ent_rx.at[source], device_id={"voc": source},
        ).wait_recv()
    ent_sum[req] = functools.reduce(jnp.add, [ent[i] for i in range(nvoc)])
    for i in range(1, nreq):
        send_sum(i).start()
    for i in range(1, nreq):
        source = lax.rem(req + i, nreq)
        pltpu.make_async_remote_copy(
            src_ref=ent_sum.at[source], dst_ref=ent_sum.at[source], send_sem=sum_tx.at[i],
            recv_sem=sum_rx.at[source], device_id={"req": source},
        ).wait_recv()
    summed = jnp.sum(functools.reduce(jnp.add, [ent_sum[i] for i in range(nreq)]), axis=-1, keepdims=True)
    mean = jnp.broadcast_to(summed[0:1] / summed[1:2], (1, slots))
    out[...] = jnp.concatenate([row_logprob, row_entropy, row_picked, mean], axis=0)

    for place in range(nz):
        for half in range(2):
            if half == 0 or 0 < place < nz - 1:
                send_side(place, half).wait_send()
            else:
                pl.when(z == place)(lambda: send_side(place, half).wait_send())
            pl.when((z > 0) & (z <= place))(lambda: send_down(place, half).wait_send())
            pl.when((z < nz - 1) & (z >= place))(lambda: send_up(place, half).wait_send())
    pl.when(z < nz - 1)(lambda: extra_up().wait_send())
    pl.when(z > 0)(lambda: extra_down().wait_send())

    for i in range(1, nvoc):
        send_meta(i).wait_send()
        send_stats(lax.rem(me + i, nvoc)).wait_send()
        send_ent(i).wait_send()
    for i in range(1, nreq):
        send_sum(i).wait_send()


def shards(nreq, nvoc, hidden, norm_gain, head, targets, bounds):
    slots, depth = hidden.shape
    width = head.shape[1]
    nz = nvoc // SIDE
    chunks = width // CHUNK
    pair = 2 * LIVE
    vmem = pl.BlockSpec(memory_space=pltpu.VMEM)
    anywhere = pl.BlockSpec(memory_space=pl.ANY)
    dma = pltpu.SemaphoreType.DMA
    out = pl.pallas_call(
        functools.partial(kernel, nreq, nvoc),
        out_shape=jax.ShapeDtypeStruct((4, slots), jnp.float32),
        in_specs=[anywhere] * 5,
        out_specs=vmem,
        scratch_shapes=[
            pltpu.VMEM((slots, depth), jnp.bfloat16),
            pltpu.VMEM((depth // LANES, LANES), jnp.float32),
            pltpu.VMEM((1, slots), jnp.int32),
            pltpu.VMEM((1, 2), jnp.int32),
            pltpu.VMEM((nvoc, LIVE, depth), jnp.bfloat16),
            pltpu.VMEM((chunks, depth, CHUNK), jnp.bfloat16),
            pltpu.VMEM((pair, CHUNK), jnp.float32),
            pltpu.VMEM((pair, CHUNK), jnp.float32),
            pltpu.VMEM((pair, LANES), jnp.float32),
            pltpu.VMEM((pair, LANES), jnp.float32),
            pltpu.VMEM((pair, LANES), jnp.float32),
            pltpu.VMEM((pair, LANES), jnp.float32),
            pltpu.VMEM((pair, LANES), jnp.int32),
            pltpu.VMEM((nvoc, 8, slots), jnp.int32),
            pltpu.VMEM((nvoc, 8, slots), jnp.float32),
            pltpu.VMEM((nvoc, 8, slots), jnp.float32),
            pltpu.VMEM((nvoc, 8, slots), jnp.float32),
            pltpu.VMEM((nreq, 8, slots), jnp.float32),
            dma((4,)),
            dma((chunks,)),
            dma((nvoc, 2)),
            dma((nz, 2)),
            dma((nz, 2)),
            dma((nz, 2)),
            dma((2,)),
            dma((nvoc,)),
            dma((nvoc,)),
            dma((nvoc,)),
            dma((nvoc,)),
            dma((nvoc,)),
            dma((nvoc,)),
            dma((nreq,)),
            dma((nreq,)),
        ],
        compiler_params=pltpu.CompilerParams(
            collective_id=0, has_side_effects=True, vmem_limit_bytes=60 * 1024 * 1024
        ),
        cost_estimate=pl.CostEstimate(
            flops=2 * nvoc * LIVE * depth * width,
            bytes_accessed=2 * depth * width,
            transcendentals=nvoc * LIVE * width,
        ),
    )(hidden, norm_gain.reshape(depth // LANES, LANES), targets.reshape(1, slots), bounds, head)
    return out[0], out[1], out[2], out[3, :1]


def solution(mesh):
    placed = (
        P(("req", "voc"), None),
        P(),
        P(None, "voc"),
        P(("req", "voc")),
        P(("req", "voc"), None),
    )
    return jax.shard_map(
        functools.partial(shards, mesh.shape["req"], mesh.shape["voc"]),
        mesh=mesh,
        in_specs=placed,
        out_specs=(P(("req", "voc")), P(("req", "voc")), P(("req", "voc")), P()),
        check_vma=False,
    )
```

```python
import functools

import jax
import jax.numpy as jnp
from jax import lax
from jax.experimental import pallas as pl
from jax.experimental.pallas import tpu as pltpu
from jax.sharding import PartitionSpec as P

LIVE = 96
HALF = LIVE // 2
SIDE = 2
LANES = 128
CHUNK = 768
PART = 256
PARTS = CHUNK // PART
TICKS = 2
LOW = -1e30


def kernel(
    nreq, nvoc, hidden_in, gain_in, targets_in, bounds_in, head, out,
    hidden, gain, targets, bounds, rows, weights, first, second, top, total, weighted, picked, group,
    meta, stats, stats_out, ent, ent_sum,
    in_sem, head_sem, rows_rx, down_tx, up_tx, side_tx, extra_tx, meta_rx, meta_tx, stats_rx, stats_tx,
    ent_rx, ent_tx, sum_rx, sum_tx,
):
    nz = nvoc // SIDE
    req = lax.axis_index("req")
    me = lax.axis_index("voc")
    x = lax.rem(me, SIDE)
    z = me // SIDE
    partner = z * SIDE + (SIDE - 1 - x)
    slots = hidden.shape[0]
    width = head.shape[1]
    chunks = width // CHUNK
    cells = CHUNK // LANES

    def at(place, side):
        return place * SIDE + side

    def load_head(c):
        return pltpu.make_async_copy(
            head.at[:, pl.ds(pl.multiple_of(c * CHUNK, CHUNK), CHUNK)], weights.at[c], head_sem.at[c]
        )

    loads = [
        pltpu.make_async_copy(source, target, in_sem.at[n])
        for n, (source, target) in enumerate(
            ((hidden_in, hidden), (gain_in, gain), (targets_in, targets), (bounds_in, bounds))
        )
    ]
    for load in loads:
        load.start()
    barrier = pltpu.get_barrier_semaphore()
    for i in range(1, nvoc):
        pl.semaphore_signal(barrier, inc=1, device_id={"voc": lax.rem(me + i, nvoc)})
    for i in range(1, nreq):
        pl.semaphore_signal(barrier, inc=1, device_id={"req": lax.rem(req + i, nreq)})

    for c in range(chunks):
        load_head(c).start()

    for load in loads:
        load.wait()
    lo = bounds[0:1, 0:1]
    hi = bounds[0:1, 1:2]
    values = hidden[...].astype(jnp.float32)
    meansq = jnp.mean(values * values, axis=-1, keepdims=True)
    values = values * lax.rsqrt(meansq + 1e-05)
    normed = jnp.concatenate(
        [values[:, j * LANES : (j + 1) * LANES] * gain[j : j + 1, :] for j in range(gain.shape[0])],
        axis=1,
    ).astype(jnp.bfloat16)
    slot = lax.broadcasted_iota(jnp.int32, (LIVE, slots), 1)
    order = lax.broadcasted_iota(jnp.int32, (LIVE, slots), 0)
    window = jnp.where(slot == order + lo, 1.0, 0.0).astype(jnp.bfloat16)
    rows[me] = jnp.dot(window, normed, preferred_element_type=jnp.float32).astype(jnp.bfloat16)
    tile_row = lax.broadcasted_iota(jnp.int32, (8, slots), 0)
    meta[me] = jnp.where(tile_row == 0, jnp.broadcast_to(targets[...], (8, slots)), jnp.broadcast_to(lo, (8, slots)))

    pl.semaphore_wait(barrier, nvoc - 1 + nreq - 1)

    def send_rows(block, half, target, sem):
        piece = rows.at[block, pl.ds(half * HALF, HALF)]
        return pltpu.make_async_remote_copy(
            src_ref=piece, dst_ref=piece, send_sem=sem,
            recv_sem=rows_rx.at[block, half], device_id={"voc": target},
        )

    def send_down(place, half):
        return send_rows(at(place, x), half, at(z - 1, x), down_tx.at[place, half])

    def send_up(place, half):
        return send_rows(at(place, x), half, at(z + 1, x), up_tx.at[place, half])

    def send_side(place, half):
        return send_rows(at(place, x), half, partner, side_tx.at[place, half])

    def extra_up():
        return send_rows(at(0, SIDE - 1 - x), 1, at(z + 1, x), extra_tx.at[0])

    def extra_down():
        return send_rows(at(nz - 1, SIDE - 1 - x), 1, at(z - 1, x), extra_tx.at[1])

    def wait_rows(block, half):
        send_rows(block, half, partner, side_tx.at[0, 0]).wait_recv()

    def send_meta(i):
        return pltpu.make_async_remote_copy(
            src_ref=meta.at[me], dst_ref=meta.at[me], send_sem=meta_tx.at[i],
            recv_sem=meta_rx.at[me], device_id={"voc": lax.rem(me + i, nvoc)},
        )

    for half in range(2):
        @pl.when(z > 0)
        def _():
            send_down(z, half).start()

        @pl.when(z < nz - 1)
        def _():
            send_up(z, half).start()

        send_side(z, half).start()
    for i in range(1, nvoc):
        send_meta(i).start()

    def local_ids(block):
        ids = jnp.broadcast_to(meta[block, 0:1, :], (LIVE, slots))
        start = jnp.broadcast_to(meta[block, 1:2, :], (LIVE, slots))
        hit = slot == order + start
        id_column = jnp.sum(jnp.where(hit, ids, 0).astype(jnp.float32), axis=-1, keepdims=True)
        return id_column.astype(jnp.int32) - me * width, hit

    def prepare(blocks):
        for n, block in enumerate(blocks):
            ids, _ = local_ids(block)
            group[pl.ds(n * LIVE, LIVE), :] = jnp.broadcast_to(ids >> 7, (LIVE, LANES))
        size = len(blocks) * LIVE
        top[pl.ds(0, size), :] = jnp.full((size, LANES), LOW, jnp.float32)
        for state in (total, weighted, picked):
            state[pl.ds(0, size), :] = jnp.zeros((size, LANES), jnp.float32)

    def multiply(blocks, c, out, n):
        left = [rows[block] for block in blocks]
        left = left[0] if len(left) == 1 else jnp.concatenate(left, axis=0)
        here = pl.ds(n * PART, PART)
        out[pl.ds(0, len(blocks) * LIVE), here] = jnp.dot(
            left, weights[c, :, here], preferred_element_type=jnp.float32
        )

    def absorb(count, c, logits, n):
        share = count * LIVE // PARTS
        for r in range(n * share, (n + 1) * share, 8):
            here = pl.ds(r, 8)
            part = [logits[here, pl.ds(j * LANES, LANES)] for j in range(cells)]
            old = top[here, :]
            new = functools.reduce(jnp.maximum, part, old)
            scale = jnp.exp(old - new)
            expo = [jnp.exp(v - new) for v in part]
            top[here, :] = new
            total[here, :] = total[here, :] * scale + functools.reduce(jnp.add, expo)
            weighted[here, :] = weighted[here, :] * scale + functools.reduce(
                jnp.add, [e * v for e, v in zip(expo, part)]
            )
            wanted = group[here, :]
            found = picked[here, :]
            for j, v in enumerate(part):
                found = jnp.where(wanted == c * cells + j, v, found)
            picked[here, :] = found

    def block_stats(n, block):
        here = pl.ds(n * LIVE, LIVE)
        ids, hit = local_ids(block)
        best = jnp.max(top[here, :], axis=-1, keepdims=True)
        scale = jnp.exp(top[here, :] - best)
        lane = lax.broadcasted_iota(jnp.int32, (LIVE, LANES), 1)
        columns = (
            best,
            jnp.sum(total[here, :] * scale, axis=-1, keepdims=True),
            jnp.sum(weighted[here, :] * scale, axis=-1, keepdims=True),
            jnp.sum(jnp.where(lane == (ids & 127), picked[here, :], 0.0), axis=-1, keepdims=True),
        )
        lines = [jnp.sum(jnp.where(hit, col, 0.0), axis=0, keepdims=True) for col in columns]
        return jnp.concatenate(lines + [jnp.zeros((4, slots), jnp.float32)], axis=0)

    def forward(t, half):
        @pl.when(z - t >= 0)
        def _():
            wait_rows(at(z - t, x), half)

            @pl.when(z < nz - 1)
            def _():
                send_up(z - t, half).start()

            @pl.when((half == 0) | (z - t > 0))
            def _():
                send_side(z - t, half).start()

        @pl.when(z + t < nz)
        def _():
            wait_rows(at(z + t, x), half)

            @pl.when(z > 0)
            def _():
                send_down(z + t, half).start()

            @pl.when((half == 0) | (z + t < nz - 1))
            def _():
                send_side(z + t, half).start()

        gap = t - 1
        if (t == 1) != (half == 1):
            return

        @pl.when(z == gap)
        def _():
            wait_rows(at(0, SIDE - 1 - x), 1)
            extra_up().start()

        @pl.when(nz - 1 - z == gap)
        def _():
            wait_rows(at(nz - 1, SIDE - 1 - x), 1)
            extra_down().start()

    def wait_across(place):
        block = at(place, SIDE - 1 - x)
        wait_rows(block, 0)
        inner = (place > 0) & (place < nz - 1)
        opposite = (place - z == nz - 1) | (z - place == nz - 1)

        @pl.when(inner | opposite)
        def _():
            wait_rows(block, 1)

    def work(blocks, fresh, events=()):
        steps = chunks // 2 - 1
        count = len(blocks)

        def ready(c):
            if fresh:
                load_head(c).wait()

        def both(c, ahead, behind):
            for n in range(PARTS):
                multiply(blocks, c, ahead, n)
                absorb(count, c - 1, behind, n)

        prepare(blocks)
        ready(0)
        for n in range(PARTS):
            multiply(blocks, 0, first, n)

        def body(i, carry):
            for when, event in events:
                if when < steps:
                    pl.when(i == when)(event)
            c = i * 2
            ready(c + 1)
            both(c + 1, second, first)
            ready(c + 2)
            both(c + 2, first, second)
            return carry

        lax.fori_loop(0, steps, body, 0)
        ready(chunks - 1)
        both(chunks - 1, second, first)
        for n in range(PARTS):
            absorb(count, chunks - 1, second, n)
        for when, event in events:
            if when >= steps:
                event()

    def send_stats(block):
        return pltpu.make_async_remote_copy(
            src_ref=stats_out.at[block], dst_ref=stats.at[me], send_sem=stats_tx.at[block],
            recv_sem=stats_rx.at[me], device_id={"voc": block},
        )

    def give(n, block):
        stats_out[block] = block_stats(n, block)
        send_stats(block).start()

    def wait_meta(block):
        pltpu.make_async_remote_copy(
            src_ref=meta.at[block], dst_ref=meta.at[block], send_sem=meta_tx.at[0],
            recv_sem=meta_rx.at[block], device_id={"voc": partner},
        ).wait_recv()

    near = jnp.minimum(z, nz - 1 - z)
    far_side = jnp.where(z > nz - 1 - z, -1, 1)

    def line(i):
        close = i < 2 * near
        step = jnp.where(close, i // 2 + 1, i - near + 1)
        side = jnp.where(close, 2 * (i % 2) - 1, far_side)
        return z + side * step

    def forwards(t):
        return [functools.partial(forward, t, half) for half in range(2)] if t < nz else []

    work([me], True, list(zip((2, chunks), forwards(1))))
    stats[me] = block_stats(0, me)

    for begin in range(1, nz, TICKS):
        end = min(begin + TICKS, nz)
        for t in range(begin + 1, end):
            for event in forwards(t):
                event()
        blocks = []
        for t in range(begin, end):
            place = z if t == 1 else line(t - 2)
            wait_across(place)
            blocks += [at(place, SIDE - 1 - x), at(line(t - 1), x)]
        if end == nz:
            wait_across(line(nz - 2))
            blocks.append(at(line(nz - 2), SIDE - 1 - x))
        for block in blocks:
            wait_meta(block)
        work(blocks, False, list(zip((1, 2), forwards(end))))
        for n, block in enumerate(blocks):
            give(n, block)

    for i in range(1, nvoc):
        source = lax.rem(me + i, nvoc)
        pltpu.make_async_remote_copy(
            src_ref=stats_out.at[source], dst_ref=stats.at[source], send_sem=stats_tx.at[source],
            recv_sem=stats_rx.at[source], device_id={"voc": source},
        ).wait_recv()
    tiles = [stats[i] for i in range(nvoc)]
    best = functools.reduce(jnp.maximum, [tile[0:1] for tile in tiles])
    scales = [jnp.exp(tile[0:1] - best) for tile in tiles]
    all_total = functools.reduce(jnp.add, [tile[1:2] * s for tile, s in zip(tiles, scales)])
    all_weighted = functools.reduce(jnp.add, [tile[2:3] * s for tile, s in zip(tiles, scales)])
    chosen = functools.reduce(jnp.add, [tile[3:4] for tile in tiles])
    place = lax.broadcasted_iota(jnp.int32, (1, slots), 1)
    live = (place >= lo) & (place < hi)
    lse = best + jnp.log(all_total)
    row_entropy = jnp.where(live, lse - all_weighted / all_total, 0.0)
    row_logprob = jnp.where(live, chosen - lse, 0.0)
    row_picked = jnp.where(live, chosen, 0.0)

    ent[me] = jnp.concatenate(
        [row_entropy, jnp.where(live, 1.0, 0.0), jnp.zeros((6, slots), jnp.float32)], axis=0
    )

    def send_ent(i):
        return pltpu.make_async_remote_copy(
            src_ref=ent.at[me], dst_ref=ent.at[me], send_sem=ent_tx.at[i],
            recv_sem=ent_rx.at[me], device_id={"voc": lax.rem(me + i, nvoc)},
        )

    def send_sum(i):
        return pltpu.make_async_remote_copy(
            src_ref=ent_sum.at[req], dst_ref=ent_sum.at[req], send_sem=sum_tx.at[i],
            recv_sem=sum_rx.at[req], device_id={"req": lax.rem(req + i, nreq)},
        )

    for i in range(1, nvoc):
        send_ent(i).start()
    for i in range(1, nvoc):
        source = lax.rem(me + i, nvoc)
        pltpu.make_async_remote_copy(
            src_ref=ent.at[source], dst_ref=ent.at[source], send_sem=ent_tx.at[i],
            recv_sem=ent_rx.at[source], device_id={"voc": source},
        ).wait_recv()
    ent_sum[req] = functools.reduce(jnp.add, [ent[i] for i in range(nvoc)])
    for i in range(1, nreq):
        send_sum(i).start()
    for i in range(1, nreq):
        source = lax.rem(req + i, nreq)
        pltpu.make_async_remote_copy(
            src_ref=ent_sum.at[source], dst_ref=ent_sum.at[source], send_sem=sum_tx.at[i],
            recv_sem=sum_rx.at[source], device_id={"req": source},
        ).wait_recv()
    summed = jnp.sum(functools.reduce(jnp.add, [ent_sum[i] for i in range(nreq)]), axis=-1, keepdims=True)
    mean = jnp.broadcast_to(summed[0:1] / summed[1:2], (1, slots))
    out[...] = jnp.concatenate([row_logprob, row_entropy, row_picked, mean], axis=0)

    for place in range(nz):
        for half in range(2):
            if half == 0 or 0 < place < nz - 1:
                send_side(place, half).wait_send()
            else:
                pl.when(z == place)(lambda: send_side(place, half).wait_send())
            pl.when((z > 0) & (z <= place))(lambda: send_down(place, half).wait_send())
            pl.when((z < nz - 1) & (z >= place))(lambda: send_up(place, half).wait_send())
    pl.when(z < nz - 1)(lambda: extra_up().wait_send())
    pl.when(z > 0)(lambda: extra_down().wait_send())

    for i in range(1, nvoc):
        send_meta(i).wait_send()
        send_stats(lax.rem(me + i, nvoc)).wait_send()
        send_ent(i).wait_send()
    for i in range(1, nreq):
        send_sum(i).wait_send()


def shards(nreq, nvoc, hidden, norm_gain, head, targets, bounds):
    slots, depth = hidden.shape
    width = head.shape[1]
    nz = nvoc // SIDE
    chunks = width // CHUNK
    pair = (2 * TICKS + 1) * LIVE
    vmem = pl.BlockSpec(memory_space=pltpu.VMEM)
    anywhere = pl.BlockSpec(memory_space=pl.ANY)
    dma = pltpu.SemaphoreType.DMA
    out = pl.pallas_call(
        functools.partial(kernel, nreq, nvoc),
        out_shape=jax.ShapeDtypeStruct((4, slots), jnp.float32),
        in_specs=[anywhere] * 5,
        out_specs=vmem,
        scratch_shapes=[
            pltpu.VMEM((slots, depth), jnp.bfloat16),
            pltpu.VMEM((depth // LANES, LANES), jnp.float32),
            pltpu.VMEM((1, slots), jnp.int32),
            pltpu.VMEM((1, 2), jnp.int32),
            pltpu.VMEM((nvoc, LIVE, depth), jnp.bfloat16),
            pltpu.VMEM((chunks, depth, CHUNK), jnp.bfloat16),
            pltpu.VMEM((pair, CHUNK), jnp.float32),
            pltpu.VMEM((pair, CHUNK), jnp.float32),
            pltpu.VMEM((pair, LANES), jnp.float32),
            pltpu.VMEM((pair, LANES), jnp.float32),
            pltpu.VMEM((pair, LANES), jnp.float32),
            pltpu.VMEM((pair, LANES), jnp.float32),
            pltpu.VMEM((pair, LANES), jnp.int32),
            pltpu.VMEM((nvoc, 8, slots), jnp.int32),
            pltpu.VMEM((nvoc, 8, slots), jnp.float32),
            pltpu.VMEM((nvoc, 8, slots), jnp.float32),
            pltpu.VMEM((nvoc, 8, slots), jnp.float32),
            pltpu.VMEM((nreq, 8, slots), jnp.float32),
            dma((4,)),
            dma((chunks,)),
            dma((nvoc, 2)),
            dma((nz, 2)),
            dma((nz, 2)),
            dma((nz, 2)),
            dma((2,)),
            dma((nvoc,)),
            dma((nvoc,)),
            dma((nvoc,)),
            dma((nvoc,)),
            dma((nvoc,)),
            dma((nvoc,)),
            dma((nreq,)),
            dma((nreq,)),
        ],
        compiler_params=pltpu.CompilerParams(
            collective_id=0, has_side_effects=True, vmem_limit_bytes=60 * 1024 * 1024
        ),
        cost_estimate=pl.CostEstimate(
            flops=2 * nvoc * LIVE * depth * width,
            bytes_accessed=2 * depth * width,
            transcendentals=nvoc * LIVE * width,
        ),
    )(hidden, norm_gain.reshape(depth // LANES, LANES), targets.reshape(1, slots), bounds, head)
    return out[0], out[1], out[2], out[3, :1]


def solution(mesh):
    placed = (
        P(("req", "voc"), None),
        P(),
        P(None, "voc"),
        P(("req", "voc")),
        P(("req", "voc"), None),
    )
    return jax.shard_map(
        functools.partial(shards, mesh.shape["req"], mesh.shape["voc"]),
        mesh=mesh,
        in_specs=placed,
        out_specs=(P(("req", "voc")), P(("req", "voc")), P(("req", "voc")), P()),
        check_vma=False,
    )
```

```python
import functools

import jax
import jax.numpy as jnp
from jax import lax
from jax.experimental import pallas as pl
from jax.experimental.pallas import tpu as pltpu
from jax.sharding import PartitionSpec as P

LIVE = 96
HALF = LIVE // 2
SIDE = 2
LANES = 128
CHUNK = 768
PART = 256
PARTS = CHUNK // PART
STEP = 32
LOW = -1e30


def tree(combine, values):
    while len(values) > 1:
        pairs = [combine(a, b) for a, b in zip(values[::2], values[1::2])]
        values = pairs + values[len(pairs) * 2 :]
    return values[0]


def kernel(
    nreq, nvoc, hidden_in, gain_in, targets_in, bounds_in, head, out,
    hidden, gain, targets, bounds, rows, weights, first, second, top, total, weighted, picked, group,
    meta, stats, stats_out, ent, ent_sum,
    in_sem, head_sem, rows_rx, down_tx, up_tx, side_tx, extra_tx, meta_rx, meta_tx, stats_rx, stats_tx,
    ent_rx, ent_tx, sum_rx, sum_tx,
):
    nz = nvoc // SIDE
    req = lax.axis_index("req")
    me = lax.axis_index("voc")
    x = lax.rem(me, SIDE)
    z = me // SIDE
    partner = z * SIDE + (SIDE - 1 - x)
    slots = hidden.shape[0]
    width = head.shape[1]
    chunks = width // CHUNK
    cells = CHUNK // LANES

    def at(place, side):
        return place * SIDE + side

    def load_head(c):
        return pltpu.make_async_copy(
            head.at[:, pl.ds(pl.multiple_of(c * CHUNK, CHUNK), CHUNK)], weights.at[c], head_sem.at[c]
        )

    loads = [
        pltpu.make_async_copy(source, target, in_sem.at[n])
        for n, (source, target) in enumerate(
            ((hidden_in, hidden), (gain_in, gain), (targets_in, targets), (bounds_in, bounds))
        )
    ]
    for load in loads:
        load.start()
    barrier = pltpu.get_barrier_semaphore()
    for i in range(1, nvoc):
        pl.semaphore_signal(barrier, inc=1, device_id={"voc": lax.rem(me + i, nvoc)})
    for i in range(1, nreq):
        pl.semaphore_signal(barrier, inc=1, device_id={"req": lax.rem(req + i, nreq)})

    for c in range(chunks):
        load_head(c).start()

    for load in loads:
        load.wait()
    lo = bounds[0:1, 0:1]
    hi = bounds[0:1, 1:2]
    values = hidden[...].astype(jnp.float32)
    meansq = jnp.mean(values * values, axis=-1, keepdims=True)
    values = values * lax.rsqrt(meansq + 1e-05)
    normed = jnp.concatenate(
        [values[:, j * LANES : (j + 1) * LANES] * gain[j : j + 1, :] for j in range(gain.shape[0])],
        axis=1,
    ).astype(jnp.bfloat16)
    slot = lax.broadcasted_iota(jnp.int32, (LIVE, slots), 1)
    order = lax.broadcasted_iota(jnp.int32, (LIVE, slots), 0)
    window = jnp.where(slot == order + lo, 1.0, 0.0).astype(jnp.bfloat16)
    rows[me] = jnp.dot(window, normed, preferred_element_type=jnp.float32).astype(jnp.bfloat16)
    tile_row = lax.broadcasted_iota(jnp.int32, (8, slots), 0)
    meta[me] = jnp.where(tile_row == 0, jnp.broadcast_to(targets[...], (8, slots)), jnp.broadcast_to(lo, (8, slots)))

    pl.semaphore_wait(barrier, nvoc - 1 + nreq - 1)

    def send_rows(block, half, target, sem):
        piece = rows.at[block, pl.ds(half * HALF, HALF)]
        return pltpu.make_async_remote_copy(
            src_ref=piece, dst_ref=piece, send_sem=sem,
            recv_sem=rows_rx.at[block, half], device_id={"voc": target},
        )

    def send_down(place, half):
        return send_rows(at(place, x), half, at(z - 1, x), down_tx.at[place, half])

    def send_up(place, half):
        return send_rows(at(place, x), half, at(z + 1, x), up_tx.at[place, half])

    def send_side(place, half):
        return send_rows(at(place, x), half, partner, side_tx.at[place, half])

    def extra_up():
        return send_rows(at(0, SIDE - 1 - x), 1, at(z + 1, x), extra_tx.at[0])

    def extra_down():
        return send_rows(at(nz - 1, SIDE - 1 - x), 1, at(z - 1, x), extra_tx.at[1])

    def wait_rows(block, half):
        send_rows(block, half, partner, side_tx.at[0, 0]).wait_recv()

    def send_meta(i):
        return pltpu.make_async_remote_copy(
            src_ref=meta.at[me], dst_ref=meta.at[me], send_sem=meta_tx.at[i],
            recv_sem=meta_rx.at[me], device_id={"voc": lax.rem(me + i, nvoc)},
        )

    for half in range(2):
        @pl.when(z > 0)
        def _():
            send_down(z, half).start()

        @pl.when(z < nz - 1)
        def _():
            send_up(z, half).start()

        send_side(z, half).start()
    for i in range(1, nvoc):
        send_meta(i).start()

    def local_ids(block):
        ids = jnp.broadcast_to(meta[block, 0:1, :], (LIVE, slots))
        start = jnp.broadcast_to(meta[block, 1:2, :], (LIVE, slots))
        hit = slot == order + start
        id_column = jnp.sum(jnp.where(hit, ids, 0).astype(jnp.float32), axis=-1, keepdims=True)
        return id_column.astype(jnp.int32) - me * width, hit

    def prepare(blocks):
        for n, block in enumerate(blocks):
            ids, _ = local_ids(block)
            group[pl.ds(n * LIVE, LIVE), :] = jnp.broadcast_to(ids >> 7, (LIVE, LANES))
        size = len(blocks) * LIVE
        top[pl.ds(0, size), :] = jnp.full((size, LANES), LOW, jnp.float32)
        for state in (total, weighted, picked):
            state[pl.ds(0, size), :] = jnp.zeros((size, LANES), jnp.float32)

    def multiply(blocks, c, out, n):
        left = [rows[block] for block in blocks]
        left = left[0] if len(left) == 1 else jnp.concatenate(left, axis=0)
        here = pl.ds(n * PART, PART)
        out[pl.ds(0, len(blocks) * LIVE), here] = jnp.dot(
            left, weights[c, :, here], preferred_element_type=jnp.float32
        )

    def absorb(count, c, logits, n):
        share = count * LIVE // PARTS
        for r in range(n * share, (n + 1) * share, STEP):
            here = pl.ds(r, STEP)
            part = [logits[here, pl.ds(j * LANES, LANES)] for j in range(cells)]
            old = top[here, :]
            old_total = total[here, :]
            old_weighted = weighted[here, :]
            found = picked[here, :]
            wanted = group[here, :]
            new = tree(jnp.maximum, part + [old])
            scale = jnp.exp(old - new)
            expo = [jnp.exp(v - new) for v in part]
            for j, v in enumerate(part):
                found = jnp.where(wanted == c * cells + j, v, found)
            new_total = old_total * scale + tree(jnp.add, expo)
            new_weighted = old_weighted * scale + tree(jnp.add, [e * v for e, v in zip(expo, part)])
            top[here, :] = new
            total[here, :] = new_total
            weighted[here, :] = new_weighted
            picked[here, :] = found

    def block_stats(n, block):
        here = pl.ds(n * LIVE, LIVE)
        ids, hit = local_ids(block)
        best = jnp.max(top[here, :], axis=-1, keepdims=True)
        scale = jnp.exp(top[here, :] - best)
        lane = lax.broadcasted_iota(jnp.int32, (LIVE, LANES), 1)
        columns = (
            best,
            jnp.sum(total[here, :] * scale, axis=-1, keepdims=True),
            jnp.sum(weighted[here, :] * scale, axis=-1, keepdims=True),
            jnp.sum(jnp.where(lane == (ids & 127), picked[here, :], 0.0), axis=-1, keepdims=True),
        )
        lines = [jnp.sum(jnp.where(hit, col, 0.0), axis=0, keepdims=True) for col in columns]
        return jnp.concatenate(lines + [jnp.zeros((4, slots), jnp.float32)], axis=0)

    def forward(t, half):
        @pl.when(z - t >= 0)
        def _():
            wait_rows(at(z - t, x), half)

            @pl.when(z < nz - 1)
            def _():
                send_up(z - t, half).start()

            @pl.when((half == 0) | (z - t > 0))
            def _():
                send_side(z - t, half).start()

        @pl.when(z + t < nz)
        def _():
            wait_rows(at(z + t, x), half)

            @pl.when(z > 0)
            def _():
                send_down(z + t, half).start()

            @pl.when((half == 0) | (z + t < nz - 1))
            def _():
                send_side(z + t, half).start()

        gap = t - 1
        due = (t == 1) if half == 1 else (t > 1)

        @pl.when(due & (z == gap))
        def _():
            wait_rows(at(0, SIDE - 1 - x), 1)
            extra_up().start()

        @pl.when(due & (nz - 1 - z == gap))
        def _():
            wait_rows(at(nz - 1, SIDE - 1 - x), 1)
            extra_down().start()

    def wait_across(place):
        block = at(place, SIDE - 1 - x)
        wait_rows(block, 0)
        inner = (place > 0) & (place < nz - 1)
        opposite = (place - z == nz - 1) | (z - place == nz - 1)

        @pl.when(inner | opposite)
        def _():
            wait_rows(block, 1)

    def work(blocks, fresh, middle=None):
        steps = chunks // 2 - 1

        def ready(c):
            if fresh:
                load_head(c).wait()

        count = len(blocks)

        def both(c, ahead, behind):
            for n in range(PARTS):
                multiply(blocks, c, ahead, n)
                absorb(count, c - 1, behind, n)

        prepare(blocks)
        ready(0)
        for n in range(PARTS):
            multiply(blocks, 0, first, n)

        def body(i, carry):
            if middle is not None:
                pl.when(i == min(2, steps - 1))(middle)
            c = i * 2
            ready(c + 1)
            both(c + 1, second, first)
            ready(c + 2)
            both(c + 2, first, second)
            return carry

        lax.fori_loop(0, steps, body, 0)
        ready(chunks - 1)
        both(chunks - 1, second, first)
        for n in range(PARTS):
            absorb(count, chunks - 1, second, n)

    def send_stats(block):
        return pltpu.make_async_remote_copy(
            src_ref=stats_out.at[block], dst_ref=stats.at[me], send_sem=stats_tx.at[block],
            recv_sem=stats_rx.at[me], device_id={"voc": block},
        )

    def give(n, block):
        stats_out[block] = block_stats(n, block)
        send_stats(block).start()

    def wait_meta(block):
        pltpu.make_async_remote_copy(
            src_ref=meta.at[block], dst_ref=meta.at[block], send_sem=meta_tx.at[0],
            recv_sem=meta_rx.at[block], device_id={"voc": partner},
        ).wait_recv()

    near = jnp.minimum(z, nz - 1 - z)
    far_side = jnp.where(z > nz - 1 - z, -1, 1)

    def line(i):
        close = i < 2 * near
        step = jnp.where(close, i // 2 + 1, i - near + 1)
        side = jnp.where(close, 2 * lax.rem(i, 2) - 1, far_side)
        return z + side * step

    work([me], True, lambda: forward(1, 0))
    stats[me] = block_stats(0, me)
    forward(1, 1)

    def tick(t, carry):
        place = jnp.where(t == 1, z, line(jnp.maximum(t - 2, 0)))
        across = at(place, SIDE - 1 - x)
        along = at(line(t - 1), x)
        wait_across(place)
        wait_meta(across)
        wait_meta(along)

        def middle():
            @pl.when(t + 1 < nz)
            def _():
                forward(t + 1, 0)

        work([across, along], False, middle)

        @pl.when(t + 1 < nz)
        def _():
            forward(t + 1, 1)

        give(0, across)
        give(1, along)
        return carry

    lax.fori_loop(1, nz, tick, 0)
    last = at(line(nz - 2), SIDE - 1 - x)
    wait_across(line(nz - 2))
    wait_meta(last)
    work([last], False)
    give(0, last)

    for i in range(1, nvoc):
        source = lax.rem(me + i, nvoc)
        pltpu.make_async_remote_copy(
            src_ref=stats_out.at[source], dst_ref=stats.at[source], send_sem=stats_tx.at[source],
            recv_sem=stats_rx.at[source], device_id={"voc": source},
        ).wait_recv()
    tiles = [stats[i] for i in range(nvoc)]
    best = functools.reduce(jnp.maximum, [tile[0:1] for tile in tiles])
    scales = [jnp.exp(tile[0:1] - best) for tile in tiles]
    all_total = functools.reduce(jnp.add, [tile[1:2] * s for tile, s in zip(tiles, scales)])
    all_weighted = functools.reduce(jnp.add, [tile[2:3] * s for tile, s in zip(tiles, scales)])
    chosen = functools.reduce(jnp.add, [tile[3:4] for tile in tiles])
    place = lax.broadcasted_iota(jnp.int32, (1, slots), 1)
    live = (place >= lo) & (place < hi)
    lse = best + jnp.log(all_total)
    row_entropy = jnp.where(live, lse - all_weighted / all_total, 0.0)
    row_logprob = jnp.where(live, chosen - lse, 0.0)
    row_picked = jnp.where(live, chosen, 0.0)

    ent[me] = jnp.concatenate(
        [row_entropy, jnp.where(live, 1.0, 0.0), jnp.zeros((6, slots), jnp.float32)], axis=0
    )

    def send_ent(i):
        return pltpu.make_async_remote_copy(
            src_ref=ent.at[me], dst_ref=ent.at[me], send_sem=ent_tx.at[i],
            recv_sem=ent_rx.at[me], device_id={"voc": lax.rem(me + i, nvoc)},
        )

    def send_sum(i):
        return pltpu.make_async_remote_copy(
            src_ref=ent_sum.at[req], dst_ref=ent_sum.at[req], send_sem=sum_tx.at[i],
            recv_sem=sum_rx.at[req], device_id={"req": lax.rem(req + i, nreq)},
        )

    for i in range(1, nvoc):
        send_ent(i).start()
    for i in range(1, nvoc):
        source = lax.rem(me + i, nvoc)
        pltpu.make_async_remote_copy(
            src_ref=ent.at[source], dst_ref=ent.at[source], send_sem=ent_tx.at[i],
            recv_sem=ent_rx.at[source], device_id={"voc": source},
        ).wait_recv()
    ent_sum[req] = functools.reduce(jnp.add, [ent[i] for i in range(nvoc)])
    for i in range(1, nreq):
        send_sum(i).start()
    for i in range(1, nreq):
        source = lax.rem(req + i, nreq)
        pltpu.make_async_remote_copy(
            src_ref=ent_sum.at[source], dst_ref=ent_sum.at[source], send_sem=sum_tx.at[i],
            recv_sem=sum_rx.at[source], device_id={"req": source},
        ).wait_recv()
    summed = jnp.sum(functools.reduce(jnp.add, [ent_sum[i] for i in range(nreq)]), axis=-1, keepdims=True)
    mean = jnp.broadcast_to(summed[0:1] / summed[1:2], (1, slots))
    out[...] = jnp.concatenate([row_logprob, row_entropy, row_picked, mean], axis=0)

    for place in range(nz):
        for half in range(2):
            if half == 0 or 0 < place < nz - 1:
                send_side(place, half).wait_send()
            else:
                pl.when(z == place)(lambda: send_side(place, half).wait_send())
            pl.when((z > 0) & (z <= place))(lambda: send_down(place, half).wait_send())
            pl.when((z < nz - 1) & (z >= place))(lambda: send_up(place, half).wait_send())
    pl.when(z < nz - 1)(lambda: extra_up().wait_send())
    pl.when(z > 0)(lambda: extra_down().wait_send())

    for i in range(1, nvoc):
        send_meta(i).wait_send()
        send_stats(lax.rem(me + i, nvoc)).wait_send()
        send_ent(i).wait_send()
    for i in range(1, nreq):
        send_sum(i).wait_send()


def shards(nreq, nvoc, hidden, norm_gain, head, targets, bounds):
    slots, depth = hidden.shape
    width = head.shape[1]
    nz = nvoc // SIDE
    chunks = width // CHUNK
    pair = 2 * LIVE
    vmem = pl.BlockSpec(memory_space=pltpu.VMEM)
    anywhere = pl.BlockSpec(memory_space=pl.ANY)
    dma = pltpu.SemaphoreType.DMA
    out = pl.pallas_call(
        functools.partial(kernel, nreq, nvoc),
        out_shape=jax.ShapeDtypeStruct((4, slots), jnp.float32),
        in_specs=[anywhere] * 5,
        out_specs=vmem,
        scratch_shapes=[
            pltpu.VMEM((slots, depth), jnp.bfloat16),
            pltpu.VMEM((depth // LANES, LANES), jnp.float32),
            pltpu.VMEM((1, slots), jnp.int32),
            pltpu.VMEM((1, 2), jnp.int32),
            pltpu.VMEM((nvoc, LIVE, depth), jnp.bfloat16),
            pltpu.VMEM((chunks, depth, CHUNK), jnp.bfloat16),
            pltpu.VMEM((pair, CHUNK), jnp.float32),
            pltpu.VMEM((pair, CHUNK), jnp.float32),
            pltpu.VMEM((pair, LANES), jnp.float32),
            pltpu.VMEM((pair, LANES), jnp.float32),
            pltpu.VMEM((pair, LANES), jnp.float32),
            pltpu.VMEM((pair, LANES), jnp.float32),
            pltpu.VMEM((pair, LANES), jnp.int32),
            pltpu.VMEM((nvoc, 8, slots), jnp.int32),
            pltpu.VMEM((nvoc, 8, slots), jnp.float32),
            pltpu.VMEM((nvoc, 8, slots), jnp.float32),
            pltpu.VMEM((nvoc, 8, slots), jnp.float32),
            pltpu.VMEM((nreq, 8, slots), jnp.float32),
            dma((4,)),
            dma((chunks,)),
            dma((nvoc, 2)),
            dma((nz, 2)),
            dma((nz, 2)),
            dma((nz, 2)),
            dma((2,)),
            dma((nvoc,)),
            dma((nvoc,)),
            dma((nvoc,)),
            dma((nvoc,)),
            dma((nvoc,)),
            dma((nvoc,)),
            dma((nreq,)),
            dma((nreq,)),
        ],
        compiler_params=pltpu.CompilerParams(
            collective_id=0, has_side_effects=True, vmem_limit_bytes=60 * 1024 * 1024
        ),
        cost_estimate=pl.CostEstimate(
            flops=2 * nvoc * LIVE * depth * width,
            bytes_accessed=2 * depth * width,
            transcendentals=nvoc * LIVE * width,
        ),
    )(hidden, norm_gain.reshape(depth // LANES, LANES), targets.reshape(1, slots), bounds, head)
    return out[0], out[1], out[2], out[3, :1]


def solution(mesh):
    placed = (
        P(("req", "voc"), None),
        P(),
        P(None, "voc"),
        P(("req", "voc")),
        P(("req", "voc"), None),
    )
    return jax.shard_map(
        functools.partial(shards, mesh.shape["req"], mesh.shape["voc"]),
        mesh=mesh,
        in_specs=placed,
        out_specs=(P(("req", "voc")), P(("req", "voc")), P(("req", "voc")), P()),
        check_vma=False,
    )
```

```python
import functools

import jax
import jax.numpy as jnp
from jax import lax
from jax.experimental import pallas as pl
from jax.experimental.pallas import tpu as pltpu
from jax.sharding import PartitionSpec as P

LIVE = 96
HALF = LIVE // 2
SIDE = 2
LANES = 128
CHUNK = 768
PART = 256
PARTS = CHUNK // PART
STEP = 32
LOW = -1e30


def tree(combine, values):
    while len(values) > 1:
        pairs = [combine(a, b) for a, b in zip(values[::2], values[1::2])]
        values = pairs + values[len(pairs) * 2 :]
    return values[0]


def kernel(
    nreq, nvoc, hidden_in, gain_in, targets_in, bounds_in, head, out,
    hidden, gain, targets, bounds, rows, weights, first, second, top, total, weighted, picked, group,
    meta, stats, stats_out, ent, ent_sum,
    in_sem, head_sem, rows_rx, down_tx, up_tx, side_tx, meta_rx, meta_tx, stats_rx, stats_tx,
    ent_rx, ent_tx, sum_rx, sum_tx,
):
    nz = nvoc // SIDE
    req = lax.axis_index("req")
    me = lax.axis_index("voc")
    x = lax.rem(me, SIDE)
    z = me // SIDE
    partner = z * SIDE + (SIDE - 1 - x)
    slots = hidden.shape[0]
    width = head.shape[1]
    chunks = width // CHUNK
    cells = CHUNK // LANES

    def at(place, side):
        return place * SIDE + side

    def load_head(c):
        return pltpu.make_async_copy(
            head.at[:, pl.ds(pl.multiple_of(c * CHUNK, CHUNK), CHUNK)], weights.at[c], head_sem.at[c]
        )

    loads = [
        pltpu.make_async_copy(source, target, in_sem.at[n])
        for n, (source, target) in enumerate(
            ((hidden_in, hidden), (gain_in, gain), (targets_in, targets), (bounds_in, bounds))
        )
    ]
    for load in loads:
        load.start()
    barrier = pltpu.get_barrier_semaphore()
    for i in range(1, nvoc):
        pl.semaphore_signal(barrier, inc=1, device_id={"voc": lax.rem(me + i, nvoc)})
    for i in range(1, nreq):
        pl.semaphore_signal(barrier, inc=1, device_id={"req": lax.rem(req + i, nreq)})

    for c in range(chunks):
        load_head(c).start()

    for load in loads:
        load.wait()
    lo = bounds[0:1, 0:1]
    hi = bounds[0:1, 1:2]
    values = hidden[...].astype(jnp.float32)
    meansq = jnp.mean(values * values, axis=-1, keepdims=True)
    values = values * lax.rsqrt(meansq + 1e-05)
    normed = jnp.concatenate(
        [values[:, j * LANES : (j + 1) * LANES] * gain[j : j + 1, :] for j in range(gain.shape[0])],
        axis=1,
    ).astype(jnp.bfloat16)
    slot = lax.broadcasted_iota(jnp.int32, (LIVE, slots), 1)
    order = lax.broadcasted_iota(jnp.int32, (LIVE, slots), 0)
    window = jnp.where(slot == order + lo, 1.0, 0.0).astype(jnp.bfloat16)
    rows[me] = jnp.dot(window, normed, preferred_element_type=jnp.float32).astype(jnp.bfloat16)
    tile_row = lax.broadcasted_iota(jnp.int32, (8, slots), 0)
    meta[me] = jnp.where(tile_row == 0, jnp.broadcast_to(targets[...], (8, slots)), jnp.broadcast_to(lo, (8, slots)))

    pl.semaphore_wait(barrier, nvoc - 1 + nreq - 1)

    def send_rows(block, half, target, sem):
        piece = rows.at[block, pl.ds(half * HALF, HALF)]
        return pltpu.make_async_remote_copy(
            src_ref=piece, dst_ref=piece, send_sem=sem,
            recv_sem=rows_rx.at[block, half], device_id={"voc": target},
        )

    def send_down(far, half):
        return send_rows(me, half, at(z - far, x), down_tx.at[far, half])

    def send_up(far, half):
        return send_rows(me, half, at(z + far, x), up_tx.at[far, half])

    def send_side(place, half):
        return send_rows(at(place, x), half, partner, side_tx.at[place, half])

    def wait_rows(block, half):
        send_rows(block, half, partner, side_tx.at[0, 0]).wait_recv()

    def send_meta(i):
        return pltpu.make_async_remote_copy(
            src_ref=meta.at[me], dst_ref=meta.at[me], send_sem=meta_tx.at[i],
            recv_sem=meta_rx.at[me], device_id={"voc": lax.rem(me + i, nvoc)},
        )

    for far in range(1, nz):
        for half in range(2):
            pl.when(z >= far)(lambda: send_down(far, half).start())
            pl.when(z + far < nz)(lambda: send_up(far, half).start())
            if far == 1:
                send_side(z, half).start()
    for i in range(1, nvoc):
        send_meta(i).start()

    def local_ids(block):
        ids = jnp.broadcast_to(meta[block, 0:1, :], (LIVE, slots))
        start = jnp.broadcast_to(meta[block, 1:2, :], (LIVE, slots))
        hit = slot == order + start
        id_column = jnp.sum(jnp.where(hit, ids, 0).astype(jnp.float32), axis=-1, keepdims=True)
        return id_column.astype(jnp.int32) - me * width, hit

    def prepare(blocks):
        for n, block in enumerate(blocks):
            ids, _ = local_ids(block)
            group[pl.ds(n * LIVE, LIVE), :] = jnp.broadcast_to(ids >> 7, (LIVE, LANES))
        size = len(blocks) * LIVE
        top[pl.ds(0, size), :] = jnp.full((size, LANES), LOW, jnp.float32)
        for state in (total, weighted, picked):
            state[pl.ds(0, size), :] = jnp.zeros((size, LANES), jnp.float32)

    def multiply(blocks, c, out, n):
        left = [rows[block] for block in blocks]
        left = left[0] if len(left) == 1 else jnp.concatenate(left, axis=0)
        here = pl.ds(n * PART, PART)
        out[pl.ds(0, len(blocks) * LIVE), here] = jnp.dot(
            left, weights[c, :, here], preferred_element_type=jnp.float32
        )

    def absorb(count, c, logits, n):
        share = count * LIVE // PARTS
        for r in range(n * share, (n + 1) * share, STEP):
            here = pl.ds(r, STEP)
            part = [logits[here, pl.ds(j * LANES, LANES)] for j in range(cells)]
            old = top[here, :]
            old_total = total[here, :]
            old_weighted = weighted[here, :]
            found = picked[here, :]
            wanted = group[here, :]
            new = tree(jnp.maximum, part + [old])
            scale = jnp.exp(old - new)
            expo = [jnp.exp(v - new) for v in part]
            for j, v in enumerate(part):
                found = jnp.where(wanted == c * cells + j, v, found)
            new_total = old_total * scale + tree(jnp.add, expo)
            new_weighted = old_weighted * scale + tree(jnp.add, [e * v for e, v in zip(expo, part)])
            top[here, :] = new
            total[here, :] = new_total
            weighted[here, :] = new_weighted
            picked[here, :] = found

    def block_stats(n, block):
        here = pl.ds(n * LIVE, LIVE)
        ids, hit = local_ids(block)
        best = jnp.max(top[here, :], axis=-1, keepdims=True)
        scale = jnp.exp(top[here, :] - best)
        lane = lax.broadcasted_iota(jnp.int32, (LIVE, LANES), 1)
        columns = (
            best,
            jnp.sum(total[here, :] * scale, axis=-1, keepdims=True),
            jnp.sum(weighted[here, :] * scale, axis=-1, keepdims=True),
            jnp.sum(jnp.where(lane == (ids & 127), picked[here, :], 0.0), axis=-1, keepdims=True),
        )
        lines = [jnp.sum(jnp.where(hit, col, 0.0), axis=0, keepdims=True) for col in columns]
        return jnp.concatenate(lines + [jnp.zeros((4, slots), jnp.float32)], axis=0)

    def forward(t, half):
        @pl.when(z - t >= 0)
        def _():
            wait_rows(at(z - t, x), half)
            send_side(z - t, half).start()

        @pl.when(z + t < nz)
        def _():
            wait_rows(at(z + t, x), half)
            send_side(z + t, half).start()

    def wait_across(place):
        for half in range(2):
            wait_rows(at(place, SIDE - 1 - x), half)

    def work(blocks, fresh, middle=None):
        steps = chunks // 2 - 1

        def ready(c):
            if fresh:
                load_head(c).wait()

        count = len(blocks)

        def both(c, ahead, behind):
            for n in range(PARTS):
                multiply(blocks, c, ahead, n)
                absorb(count, c - 1, behind, n)

        prepare(blocks)
        ready(0)
        for n in range(PARTS):
            multiply(blocks, 0, first, n)

        def body(i, carry):
            if middle is not None:
                pl.when(i == min(2, steps - 1))(middle)
            c = i * 2
            ready(c + 1)
            both(c + 1, second, first)
            ready(c + 2)
            both(c + 2, first, second)
            return carry

        lax.fori_loop(0, steps, body, 0)
        ready(chunks - 1)
        both(chunks - 1, second, first)
        for n in range(PARTS):
            absorb(count, chunks - 1, second, n)

    def send_stats(block):
        return pltpu.make_async_remote_copy(
            src_ref=stats_out.at[block], dst_ref=stats.at[me], send_sem=stats_tx.at[block],
            recv_sem=stats_rx.at[me], device_id={"voc": block},
        )

    def give(n, block):
        stats_out[block] = block_stats(n, block)
        send_stats(block).start()

    def wait_meta(block):
        pltpu.make_async_remote_copy(
            src_ref=meta.at[block], dst_ref=meta.at[block], send_sem=meta_tx.at[0],
            recv_sem=meta_rx.at[block], device_id={"voc": partner},
        ).wait_recv()

    near = jnp.minimum(z, nz - 1 - z)
    far_side = jnp.where(z > nz - 1 - z, -1, 1)

    def line(i):
        close = i < 2 * near
        step = jnp.where(close, i // 2 + 1, i - near + 1)
        side = jnp.where(close, 2 * lax.rem(i, 2) - 1, far_side)
        return z + side * step

    work([me], True, lambda: forward(1, 0))
    stats[me] = block_stats(0, me)
    forward(1, 1)

    def tick(t, carry):
        place = jnp.where(t == 1, z, line(jnp.maximum(t - 2, 0)))
        across = at(place, SIDE - 1 - x)
        along = at(line(t - 1), x)
        wait_across(place)
        wait_meta(across)
        wait_meta(along)

        def middle():
            @pl.when(t + 1 < nz)
            def _():
                forward(t + 1, 0)

        work([across, along], False, middle)

        @pl.when(t + 1 < nz)
        def _():
            forward(t + 1, 1)

        give(0, across)
        give(1, along)
        return carry

    lax.fori_loop(1, nz, tick, 0)
    last = at(line(nz - 2), SIDE - 1 - x)
    wait_across(line(nz - 2))
    wait_meta(last)
    work([last], False)
    give(0, last)

    for i in range(1, nvoc):
        source = lax.rem(me + i, nvoc)
        pltpu.make_async_remote_copy(
            src_ref=stats_out.at[source], dst_ref=stats.at[source], send_sem=stats_tx.at[source],
            recv_sem=stats_rx.at[source], device_id={"voc": source},
        ).wait_recv()
    tiles = [stats[i] for i in range(nvoc)]
    best = functools.reduce(jnp.maximum, [tile[0:1] for tile in tiles])
    scales = [jnp.exp(tile[0:1] - best) for tile in tiles]
    all_total = functools.reduce(jnp.add, [tile[1:2] * s for tile, s in zip(tiles, scales)])
    all_weighted = functools.reduce(jnp.add, [tile[2:3] * s for tile, s in zip(tiles, scales)])
    chosen = functools.reduce(jnp.add, [tile[3:4] for tile in tiles])
    place = lax.broadcasted_iota(jnp.int32, (1, slots), 1)
    live = (place >= lo) & (place < hi)
    lse = best + jnp.log(all_total)
    row_entropy = jnp.where(live, lse - all_weighted / all_total, 0.0)
    row_logprob = jnp.where(live, chosen - lse, 0.0)
    row_picked = jnp.where(live, chosen, 0.0)

    ent[me] = jnp.concatenate(
        [row_entropy, jnp.where(live, 1.0, 0.0), jnp.zeros((6, slots), jnp.float32)], axis=0
    )

    def send_ent(i):
        return pltpu.make_async_remote_copy(
            src_ref=ent.at[me], dst_ref=ent.at[me], send_sem=ent_tx.at[i],
            recv_sem=ent_rx.at[me], device_id={"voc": lax.rem(me + i, nvoc)},
        )

    def send_sum(i):
        return pltpu.make_async_remote_copy(
            src_ref=ent_sum.at[req], dst_ref=ent_sum.at[req], send_sem=sum_tx.at[i],
            recv_sem=sum_rx.at[req], device_id={"req": lax.rem(req + i, nreq)},
        )

    for i in range(1, nvoc):
        send_ent(i).start()
    for i in range(1, nvoc):
        source = lax.rem(me + i, nvoc)
        pltpu.make_async_remote_copy(
            src_ref=ent.at[source], dst_ref=ent.at[source], send_sem=ent_tx.at[i],
            recv_sem=ent_rx.at[source], device_id={"voc": source},
        ).wait_recv()
    ent_sum[req] = functools.reduce(jnp.add, [ent[i] for i in range(nvoc)])
    for i in range(1, nreq):
        send_sum(i).start()
    for i in range(1, nreq):
        source = lax.rem(req + i, nreq)
        pltpu.make_async_remote_copy(
            src_ref=ent_sum.at[source], dst_ref=ent_sum.at[source], send_sem=sum_tx.at[i],
            recv_sem=sum_rx.at[source], device_id={"req": source},
        ).wait_recv()
    summed = jnp.sum(functools.reduce(jnp.add, [ent_sum[i] for i in range(nreq)]), axis=-1, keepdims=True)
    mean = jnp.broadcast_to(summed[0:1] / summed[1:2], (1, slots))
    out[...] = jnp.concatenate([row_logprob, row_entropy, row_picked, mean], axis=0)

    for half in range(2):
        for place in range(nz):
            send_side(place, half).wait_send()
        for far in range(1, nz):
            pl.when(z >= far)(lambda: send_down(far, half).wait_send())
            pl.when(z + far < nz)(lambda: send_up(far, half).wait_send())

    for i in range(1, nvoc):
        send_meta(i).wait_send()
        send_stats(lax.rem(me + i, nvoc)).wait_send()
        send_ent(i).wait_send()
    for i in range(1, nreq):
        send_sum(i).wait_send()


def shards(nreq, nvoc, hidden, norm_gain, head, targets, bounds):
    slots, depth = hidden.shape
    width = head.shape[1]
    nz = nvoc // SIDE
    chunks = width // CHUNK
    pair = 2 * LIVE
    vmem = pl.BlockSpec(memory_space=pltpu.VMEM)
    anywhere = pl.BlockSpec(memory_space=pl.ANY)
    dma = pltpu.SemaphoreType.DMA
    out = pl.pallas_call(
        functools.partial(kernel, nreq, nvoc),
        out_shape=jax.ShapeDtypeStruct((4, slots), jnp.float32),
        in_specs=[anywhere] * 5,
        out_specs=vmem,
        scratch_shapes=[
            pltpu.VMEM((slots, depth), jnp.bfloat16),
            pltpu.VMEM((depth // LANES, LANES), jnp.float32),
            pltpu.VMEM((1, slots), jnp.int32),
            pltpu.VMEM((1, 2), jnp.int32),
            pltpu.VMEM((nvoc, LIVE, depth), jnp.bfloat16),
            pltpu.VMEM((chunks, depth, CHUNK), jnp.bfloat16),
            pltpu.VMEM((pair, CHUNK), jnp.float32),
            pltpu.VMEM((pair, CHUNK), jnp.float32),
            pltpu.VMEM((pair, LANES), jnp.float32),
            pltpu.VMEM((pair, LANES), jnp.float32),
            pltpu.VMEM((pair, LANES), jnp.float32),
            pltpu.VMEM((pair, LANES), jnp.float32),
            pltpu.VMEM((pair, LANES), jnp.int32),
            pltpu.VMEM((nvoc, 8, slots), jnp.int32),
            pltpu.VMEM((nvoc, 8, slots), jnp.float32),
            pltpu.VMEM((nvoc, 8, slots), jnp.float32),
            pltpu.VMEM((nvoc, 8, slots), jnp.float32),
            pltpu.VMEM((nreq, 8, slots), jnp.float32),
            dma((4,)),
            dma((chunks,)),
            dma((nvoc, 2)),
            dma((nz, 2)),
            dma((nz, 2)),
            dma((nz, 2)),
            dma((nvoc,)),
            dma((nvoc,)),
            dma((nvoc,)),
            dma((nvoc,)),
            dma((nvoc,)),
            dma((nvoc,)),
            dma((nreq,)),
            dma((nreq,)),
        ],
        compiler_params=pltpu.CompilerParams(
            collective_id=0, has_side_effects=True, vmem_limit_bytes=60 * 1024 * 1024
        ),
        cost_estimate=pl.CostEstimate(
            flops=2 * nvoc * LIVE * depth * width,
            bytes_accessed=2 * depth * width,
            transcendentals=nvoc * LIVE * width,
        ),
    )(hidden, norm_gain.reshape(depth // LANES, LANES), targets.reshape(1, slots), bounds, head)
    return out[0], out[1], out[2], out[3, :1]


def solution(mesh):
    placed = (
        P(("req", "voc"), None),
        P(),
        P(None, "voc"),
        P(("req", "voc")),
        P(("req", "voc"), None),
    )
    return jax.shard_map(
        functools.partial(shards, mesh.shape["req"], mesh.shape["voc"]),
        mesh=mesh,
        in_specs=placed,
        out_specs=(P(("req", "voc")), P(("req", "voc")), P(("req", "voc")), P()),
        check_vma=False,
    )
```
